128 devices in a mesh: pb: 4 (over z_hi, core), kv: 32 (over y, x, z_lo).
Axes of the slice: x: 4, y: 4, z: 4 (z_hi: 2, z_lo: 2; z = z_hi * 2 + z_lo), core: 2. Of those that a mesh axis runs over, the one named last changes fastest.
Arguments:
- queries: bfloat16 [131072, 256], P(('pb', 'kv')), may hold values from -64 to 64
- keys: bfloat16 [4096, 256], P('kv'), may hold values from -6 to 6
- values: bfloat16 [4096, 256], P('kv'), may hold values from -6 to 6
- dout: bfloat16 [131072, 256], P(('pb', 'kv')), may hold values from -256 to 256
Outputs:
- dq: float32 [131072, 256], P(('pb', 'kv'))
- dk: float32 [4096, 256], P('kv')
- dv: float32 [4096, 256], P('kv')
The draws below stay inside these ranges and needn't reach their ends.
All inputs are finite; a program needn't handle non-finite values.
Results may differ from the reference program's by a relative error of at most 0.0029.
Values may be sent and summed in bfloat16 or wider, within the bound.
A program may use at most 64 MiB of HBM per device.

```python
import math
import jax
import jax.numpy as jnp
from jax import lax

H = 2
DH = 128
TQ = 131072
TK = 4096


def paired(key):
    key_draw = jax.random.fold_in(key, 101)
    query_draw = jax.random.fold_in(key, 202)
    keys_arr = jnp.clip(jax.random.normal(key_draw, (TK, H * DH), jnp.float32), -6.0, 6.0)
    queries_arr = jnp.clip(jax.random.normal(query_draw, (TQ, H * DH), jnp.float32), -6.0, 6.0)
    return (queries_arr, keys_arr)


def draw_queries(key, part):
    return paired(key)[0].astype(jnp.bfloat16)


def draw_keys(key, part):
    return paired(key)[1].astype(jnp.bfloat16)


def block_scale(key, shape, split, smallest, largest):
    level = 1.0
    for axis_at, shards_of in split:
        steps = jax.random.uniform(jax.random.fold_in(jax.random.fold_in(key, 6), axis_at), (shards_of,), jnp.float32, smallest / len(split), largest / len(split))
        level = level * jnp.repeat(jnp.exp(steps), shape[axis_at] // shards_of).reshape((-1,) + (1,) * (len(shape) - 1 - axis_at))
    return level


def gaussian(rng, dims, width, bound, split=(), dtype=jnp.bfloat16):
    array = width * jax.random.normal(rng, dims, jnp.float32)
    if split:
        array = array * block_scale(rng, dims, split, -0.22, 0.18)
    return jnp.clip(array, -bound, bound).astype(dtype)


def setup_inputs(seed: int = 0) -> dict:
    splits = jax.random.split(jax.random.key(seed), 5)
    queries = draw_queries(jax.random.fold_in(splits[4], 71), 0)
    keys = draw_keys(jax.random.fold_in(splits[4], 71), 0)
    values = gaussian(splits[2], (TK, H * DH), 1.0, 6.0, ((0, 32),))
    dout = gaussian(splits[3], (TQ, H * DH), 48.0, 256.0, ((0, 128),))
    return dict(queries=queries, keys=keys, values=values, dout=dout)


def reference(queries, keys, values, dout):
    score_scale = 1.0 / math.sqrt(DH)
    block_rows = math.gcd(TQ, 2048)
    blocks = TQ // block_rows
    key_heads = keys.astype(jnp.float32).reshape(TK, H, DH)
    value_heads = values.astype(jnp.float32).reshape(TK, H, DH)
    query_blocks = queries.astype(jnp.float32).reshape(blocks, block_rows, H, DH)
    grad_blocks = dout.astype(jnp.float32).reshape(blocks, block_rows, H, DH)

    def one_block(carry, pair):
        dk_total, dv_total = carry
        query_blk, grad_blk = pair
        logits = jnp.einsum('qhd,khd->hqk', query_blk, key_heads) * score_scale
        peak = lax.optimization_barrier(jnp.max(logits, axis=-1, keepdims=True))
        mass = lax.optimization_barrier(jnp.sum(jnp.exp(logits - peak), axis=-1, keepdims=True))
        lse = peak + jnp.log(mass)
        dprob = jnp.einsum('qhd,khd->hqk', grad_blk, value_heads)
        probs = jnp.exp(logits - lse)
        delta = lax.optimization_barrier(jnp.sum(probs * dprob, axis=-1, keepdims=True))
        dlogits = probs * (dprob - delta)
        probs_b = lax.optimization_barrier(probs.astype(jnp.bfloat16)).astype(jnp.float32)
        dlogits_b = lax.optimization_barrier(dlogits.astype(jnp.bfloat16)).astype(jnp.float32)
        dv_total = dv_total + jnp.einsum('hqk,qhd->khd', probs_b, grad_blk)
        dk_total = dk_total + jnp.einsum('hqk,qhd->khd', dlogits_b, query_blk) * score_scale
        dq_block = jnp.einsum('hqk,khd->qhd', dlogits_b, key_heads) * score_scale
        return ((dk_total, dv_total), dq_block)
    zeros = jnp.zeros((TK, H, DH), jnp.float32)
    (dk_total, dv_total), dq_blocks = lax.scan(one_block, (zeros, zeros), (query_blocks, grad_blocks))
    dq = dq_blocks.reshape(TQ, H * DH)
    return (dq, dk_total.reshape(TK, H * DH), dv_total.reshape(TK, H * DH))
```

```python
import functools
import math

import jax
import jax.numpy as jnp
from jax import lax
from jax.experimental import pallas as pl
from jax.experimental.pallas import tpu as pltpu
from jax.sharding import PartitionSpec as P

D = 128
SIDE = 4
CHUNK = 512
HALF = 256
SCALE = 1.0 / math.sqrt(D)
SCALE2 = SCALE * math.log2(math.e)
GRAY = (0, 1, 3, 2)
BACK = (0, 2, 1, 3)
NT = (((1,), (1,)), ((), ()))
NN = (((1,), (0,)), ((), ()))
TN = (((0,), (0,)), ((), ()))
F32 = jnp.float32
BF16 = jnp.bfloat16


def dot(a, b, dims):
    return lax.dot_general(a, b, dims, preferred_element_type=F32)


def remote(src, dst, send, recv, device):
    return pltpu.make_async_remote_copy(
        src_ref=src, dst_ref=dst, send_sem=send, recv_sem=recv,
        device_id=device, device_id_type=pl.DeviceIdType.MESH,
    )


def kernel(
    q_in, k_in, v_in, g_in, dq_out, dk_out, dv_out,
    q, g, kv, top, mass, wsum, dqt, dqs, out1, in1, acc, in2, in3, fin,
    own_sem, q_s, q_r, z_s, z_r, b_s, b_r, a_s, a_r,
    r1_s, r1_r, r2_s, r2_r, r3_s, r3_r, o_s, o_r,
):
    rows = q_in.shape[0]
    pb, kvi = lax.axis_index("pb"), lax.axis_index("kv")
    core, zh = pb % 2, pb // 2
    y, x, zl = kvi // 8, (kvi // 2) % 4, kvi % 2

    def a_peer(d):
        return (pb, (((y + d * (1 - core)) % SIDE) * SIDE + (x + d * core) % SIDE) * 2 + zl)

    def b_peer(d):
        return (pb, (((y + d * core) % SIDE) * SIDE + (x + d * (1 - core)) % SIDE) * 2 + zl)

    twin = (zh * 2 + 1 - core, kvi)
    far_z = (1 - zh) * 2 + core
    near = kvi + 1 - 2 * zl
    z_peer = (pb, near)
    z_peers = ((far_z, kvi), z_peer, (far_z, near))
    mine = pl.ds(pl.multiple_of(core * D, D), D)
    other = pl.ds(pl.multiple_of((1 - core) * D, D), D)

    def slot(sa, sb):
        return kv.at[sa * 2 + sb // 2, sb % 2]

    barrier = pltpu.get_barrier_semaphore()
    peers = [twin, *z_peers]
    peers += [a_peer(d) for d in (1, 2, 3)] + [b_peer(d) for d in (1, 2, 3)]
    for peer in peers:
        pl.semaphore_signal(barrier, inc=1, device_id=peer, device_id_type=pl.DeviceIdType.MESH)

    here = slot(0, 0)
    own = []
    for n, (src, dst) in enumerate((
        (k_in.at[:, mine], here.at[0, 0:D]),
        (v_in.at[:, mine], here.at[1, 0:D]),
        (q_in.at[:, mine], q.at[0:rows]),
        (g_in.at[:, mine], g.at[0:rows]),
    )):
        own.append(pltpu.make_async_copy(src, dst, own_sem.at[n]))
        own[-1].start()
    pl.semaphore_wait(barrier, len(peers))

    sends = []

    def go(*args):
        c = remote(*args)
        c.start()
        sends.append(c)
        return c

    own[0].wait()
    own[1].wait()
    z_copy = go(here.at[:, 0:D], here.at[:, D:HALF], z_s, z_r, z_peer)
    b_copies = {}
    for s in (1, 2, 3):
        b_copies[s, 0] = go(
            here.at[:, 0:D], slot(0, BACK[s]).at[:, 0:D],
            b_s.at[s - 1, 0], b_r.at[BACK[s] - 1, 0], b_peer(GRAY[s]),
        )
    q_copies = [
        go(q_in.at[:, other], q.at[rows : 2 * rows], q_s.at[0], q_r.at[0], twin),
        go(g_in.at[:, other], g.at[rows : 2 * rows], q_s.at[1], q_r.at[1], twin),
    ]
    top[...] = jnp.full_like(top, -1e30)
    mass[...] = jnp.zeros_like(mass)
    wsum[...] = jnp.zeros_like(wsum)
    dqt[...] = jnp.zeros_like(dqt)

    z_copy.wait_recv()
    for s in (1, 2, 3):
        b_copies[s, 1] = go(
            here.at[:, D:HALF], slot(0, BACK[s]).at[:, D:HALF],
            b_s.at[s - 1, 1], b_r.at[BACK[s] - 1, 1], b_peer(GRAY[s]),
        )

    def along_a(sb):
        for s in (1, 2, 3):
            go(
                slot(0, sb), slot(BACK[s], sb),
                a_s.at[s - 1, sb], a_r.at[BACK[s] - 1, sb], a_peer(GRAY[s]),
            )

    along_a(0)
    for sb in (1, 2, 3):
        for rz in (0, 1):
            part = slot(0, sb).at[:, rz * D : rz * D + D]
            remote(part, part, b_s.at[sb - 1, rz], b_r.at[sb - 1, rz], twin).wait_recv()
        along_a(sb)
    own[2].wait()
    own[3].wait()
    for c in q_copies:
        c.wait_recv()

    def stats(i, carry):
        @pl.when(i >= 2)
        def _():
            for n in (0, 1):
                part = kv.at[i, n]
                sem = (i // 2 - 1, (i % 2) * 2 + n)
                remote(part, part, a_s.at[sem], a_r.at[sem], twin).wait_recv()

        nq = q.shape[0]
        kc = kv[i, :, 0].reshape(CHUNK, D)
        vc = kv[i, :, 1].reshape(CHUNK, D)
        s = dot(kc, q[...], NT).reshape(CHUNK // 8, 8, nq)
        dp = dot(vc, g[...], NT).reshape(CHUNK // 8, 8, nq)
        before = top[...]
        peak = jnp.maximum(before, jnp.max(s, axis=0) * SCALE2)
        keep = jnp.exp2(before - peak)
        e = jnp.exp2(s * SCALE2 - peak[None])
        top[...] = peak
        mass[...] = mass[...] * keep + jnp.sum(e, axis=0)
        wsum[...] = wsum[...] * keep + jnp.sum(e * dp, axis=0)
        return carry

    lax.fori_loop(0, 8, stats, 0)
    peak = jnp.max(top[...], axis=0, keepdims=True)
    keep = jnp.exp2(top[...] - peak)
    total = jnp.sum(mass[...] * keep, axis=0, keepdims=True)
    weighted = jnp.sum(wsum[...] * keep, axis=0, keepdims=True)
    top[0:1] = peak + jnp.log2(total)
    wsum[0:1] = weighted / total

    def r1_copy(s, h):
        return remote(
            out1.at[s - 1, h], in1.at[BACK[s] - 1, h],
            r1_s.at[s - 1, h], r1_r.at[BACK[s] - 1, h], a_peer(GRAY[s]),
        )

    def r1_here(s, h):
        return remote(
            out1.at[s - 1, h], in1.at[s - 1, h], r1_s.at[s - 1, h], r1_r.at[s - 1, h], twin
        )

    def r2_copy(s):
        at = (s % 2) * HALF
        return remote(
            acc.at[s // 2, :, at : at + HALF], in2.at[BACK[s] - 1],
            r2_s.at[s - 1], r2_r.at[BACK[s] - 1], b_peer(GRAY[s]),
        )

    def grads(n, carry):
        i = 7 - n
        kc = kv[i, :, 0].reshape(CHUNK, D)
        vc = kv[i, :, 1].reshape(CHUNK, D)
        qq, gg = q[...], g[...]
        s = dot(kc, qq, NT)
        dp = dot(vc, gg, NT)
        p = jnp.exp2(s * SCALE2 - top[0:1])
        ds = (p * (dp - wsum[0:1])).astype(BF16)
        dv = dot(p.astype(BF16), gg, NN)
        dk = dot(ds, qq, NN) * SCALE
        dqt[...] += dot(kc, ds, TN)

        @pl.when(i >= 2)
        def _():
            out1[i // 2 - 1, i % 2, 0] = dk.astype(BF16)
            out1[i // 2 - 1, i % 2, 1] = dv.astype(BF16)

        @pl.when(i < 2)
        def _():
            acc[i % 2, 0] = dk
            acc[i % 2, 1] = dv

        for sa in (1, 2, 3):
            for h in (0, 1):
                @pl.when(i == sa * 2 + h)
                def _(sa=sa, h=h):
                    r1_copy(sa, h).start()

        @pl.when(i == 1)
        def _():
            for sa in (1, 2, 3):
                r1_here(sa, 1).wait_recv()
            acc[1] += in1[0, 1].astype(F32) + in1[1, 1].astype(F32) + in1[2, 1].astype(F32)
            r2_copy(3).start()
            r2_copy(2).start()

        return carry

    lax.fori_loop(0, 8, grads, 0)
    for sa in (1, 2, 3):
        r1_here(sa, 0).wait_recv()
    acc[0] += in1[0, 0].astype(F32) + in1[1, 0].astype(F32) + in1[2, 0].astype(F32)
    r2_copy(1).start()

    dqs[...] = dqt[...].T * SCALE
    dq_sent = go(dqs.at[rows : 2 * rows], dq_out.at[:, mine], o_s.at[0], o_r.at[0], twin)
    dq_here = pltpu.make_async_copy(dqs.at[0:rows], dq_out.at[:, mine], own_sem.at[0])
    dq_here.start()

    for s in (1, 2, 3):
        remote(in2.at[s - 1], in2.at[s - 1], r2_s.at[s - 1], r2_r.at[s - 1], twin).wait_recv()
    acc[0, :, 0:HALF] += in2[0] + in2[1] + in2[2]
    z_sums = [
        go(acc.at[0, :, at : at + D], in3.at[n], r3_s.at[n], r3_r.at[n], z_peers[n])
        for n, at in ((0, 0), (1, D), (2, D))
    ]
    for c in z_sums:
        c.wait_recv()
    fin[...] = acc[0, :, 0:D] + in3[0] + in3[1] + in3[2]
    outs = [
        go(fin.at[n], ref.at[:, mine], o_s.at[n + 1], o_r.at[n + 1], twin)
        for n, ref in enumerate((dk_out, dv_out))
    ]
    local = [
        pltpu.make_async_copy(fin.at[n], ref.at[:, mine], own_sem.at[n + 1])
        for n, ref in enumerate((dk_out, dv_out))
    ]
    for c in local:
        c.start()
    for c in (dq_here, *local):
        c.wait()
    remote(dqs.at[0:rows], dq_out.at[:, other], o_s.at[0], o_r.at[0], twin).wait_recv()
    for n, ref in enumerate((dk_out, dv_out)):
        remote(fin.at[n], ref.at[:, other], o_s.at[n + 1], o_r.at[n + 1], twin).wait_recv()
    for c in sends:
        c.wait_send()
    for s in (1, 2, 3):
        for h in (0, 1):
            r1_copy(s, h).wait_send()
        r2_copy(s).wait_send()


def local(queries, keys, values, dout):
    rows = queries.shape[0]
    key_rows = keys.shape[0]
    dma = pltpu.SemaphoreType.DMA
    vmem = pltpu.VMEM
    return pl.pallas_call(
        kernel,
        out_shape=(
            jax.ShapeDtypeStruct((rows, 2 * D), F32),
            jax.ShapeDtypeStruct((key_rows, 2 * D), F32),
            jax.ShapeDtypeStruct((key_rows, 2 * D), F32),
        ),
        in_specs=[pl.BlockSpec(memory_space=pl.ANY)] * 4,
        out_specs=[pl.BlockSpec(memory_space=pl.ANY)] * 3,
        scratch_shapes=[
            vmem((2 * rows, D), BF16),
            vmem((2 * rows, D), BF16),
            vmem((8, 2, 2, HALF, D), BF16),
            vmem((8, 2 * rows), F32),
            vmem((8, 2 * rows), F32),
            vmem((8, 2 * rows), F32),
            vmem((D, 2 * rows), F32),
            vmem((2 * rows, D), F32),
            vmem((3, 2, 2, CHUNK, D), BF16),
            vmem((3, 2, 2, CHUNK, D), BF16),
            vmem((2, 2, CHUNK, D), F32),
            vmem((3, 2, HALF, D), F32),
            vmem((3, 2, D, D), F32),
            vmem((2, D, D), F32),
            dma((4,)), dma((2,)), dma((2,)), dma, dma,
            dma((3, 2)), dma((3, 2)), dma((3, 4)), dma((3, 4)),
            dma((3, 2)), dma((3, 2)), dma((3,)), dma((3,)),
            dma((3,)), dma((3,)), dma((3,)), dma((3,)),
        ],
        compiler_params=pltpu.CompilerParams(
            collective_id=0, has_side_effects=True, vmem_limit_bytes=56 * 2**20
        ),
    )(queries, keys, values, dout)


def solution(mesh):
    return jax.shard_map(
        local,
        mesh=mesh,
        in_specs=(P(("pb", "kv"), None), P("kv", None), P("kv", None), P(("pb", "kv"), None)),
        out_specs=(P(("pb", "kv"), None), P("kv", None), P("kv", None)),
        check_vma=False,
    )
```

```python
import functools
import math

import jax
import jax.numpy as jnp
from jax import lax
from jax.experimental import pallas as pl
from jax.experimental.pallas import tpu as pltpu
from jax.sharding import PartitionSpec as P

D = 128
SIDE = 4
CHUNK = 512
HALF = 256
SCALE = 1.0 / math.sqrt(D)
SCALE2 = SCALE * math.log2(math.e)
GRAY = (0, 1, 3, 2)
BACK = (0, 2, 1, 3)
ORDER = (
    (3, 1), (1, 1), (2, 1), (3, 2), (1, 2), (2, 2), (3, 3), (1, 3),
    (2, 3), (3, 0), (0, 1), (0, 2), (0, 3), (1, 0), (2, 0), (0, 0),
)
POS = {piece: n for n, piece in enumerate(ORDER)}
STEPS = len(ORDER) // 2
PARTS = 4
NT = (((1,), (1,)), ((), ()))
NN = (((1,), (0,)), ((), ()))
TN = (((0,), (0,)), ((), ()))
F32 = jnp.float32
BF16 = jnp.bfloat16


def dot(a, b, dims):
    return lax.dot_general(a, b, dims, preferred_element_type=F32)


def remote(src, dst, send, recv, device):
    return pltpu.make_async_remote_copy(
        src_ref=src, dst_ref=dst, send_sem=send, recv_sem=recv,
        device_id=device, device_id_type=pl.DeviceIdType.MESH,
    )


def kernel(
    q_in, k_in, v_in, g_in, dq_out, dk_out, dv_out,
    q, g, kv, top, mass, wsum, ds_all, dqs, out1, in1, acc, in2, out3, in3, fin,
    own_sem, q_s, q_r, z_s, z_r, b_s, b_r, a_s, a_r,
    r1_s, r1_r, r2_s, r2_r, r3_s, r3_r, o_s, o_r,
):
    rows = q_in.shape[0]
    pb, kvi = lax.axis_index("pb"), lax.axis_index("kv")
    core, zh = pb % 2, pb // 2
    y, x, zl = kvi // 8, (kvi // 2) % 4, kvi % 2

    def a_peer(d):
        return (pb, (((y + d * (1 - core)) % SIDE) * SIDE + (x + d * core) % SIDE) * 2 + zl)

    def b_peer(d):
        return (pb, (((y + d * core) % SIDE) * SIDE + (x + d * (1 - core)) % SIDE) * 2 + zl)

    twin = (zh * 2 + 1 - core, kvi)
    far_z = (1 - zh) * 2 + core
    near = kvi + 1 - 2 * zl
    z_peer = (pb, near)
    z_peers = ((far_z, kvi), z_peer, (far_z, near))
    mine = pl.ds(pl.multiple_of(core * D, D), D)
    other = pl.ds(pl.multiple_of((1 - core) * D, D), D)

    def slot(sa, sb):
        return kv.at[POS[sa, sb]]

    barrier = pltpu.get_barrier_semaphore()
    peers = [twin, *z_peers]
    peers += [a_peer(d) for d in (1, 2, 3)] + [b_peer(d) for d in (1, 2, 3)]
    for peer in peers:
        pl.semaphore_signal(barrier, inc=1, device_id=peer, device_id_type=pl.DeviceIdType.MESH)

    here = slot(0, 0)
    own = []
    for n, (src, dst) in enumerate((
        (k_in.at[:, mine], here.at[0, 0:D]),
        (v_in.at[:, mine], here.at[1, 0:D]),
        (q_in.at[:, mine], q.at[0:rows]),
        (g_in.at[:, mine], g.at[0:rows]),
    )):
        own.append(pltpu.make_async_copy(src, dst, own_sem.at[n]))
        own[-1].start()
    pl.semaphore_wait(barrier, len(peers))

    sends = []

    def go(*args):
        c = remote(*args)
        c.start()
        sends.append(c)
        return c

    own[0].wait()
    own[1].wait()
    z_copy = go(here.at[:, 0:D], here.at[:, D:HALF], z_s, z_r, z_peer)
    b_copies = {}
    for s in (1, 2, 3):
        b_copies[s, 0] = go(
            here.at[:, 0:D], slot(0, BACK[s]).at[:, 0:D],
            b_s.at[s - 1, 0], b_r.at[BACK[s] - 1, 0], b_peer(GRAY[s]),
        )
    q_copies = [
        go(q_in.at[:, other], q.at[rows : 2 * rows], q_s.at[0], q_r.at[0], twin),
        go(g_in.at[:, other], g.at[rows : 2 * rows], q_s.at[1], q_r.at[1], twin),
    ]
    top[...] = jnp.full_like(top, -1e30)
    mass[...] = jnp.zeros_like(mass)
    wsum[...] = jnp.zeros_like(wsum)

    z_copy.wait_recv()
    for s in (1, 2, 3):
        b_copies[s, 1] = go(
            here.at[:, D:HALF], slot(0, BACK[s]).at[:, D:HALF],
            b_s.at[s - 1, 1], b_r.at[BACK[s] - 1, 1], b_peer(GRAY[s]),
        )

    def along_a(sb):
        for s in (1, 2, 3):
            go(
                slot(0, sb), slot(BACK[s], sb),
                a_s.at[POS[s, sb]], a_r.at[POS[BACK[s], sb]], a_peer(GRAY[s]),
            )

    along_a(0)
    for sb in (3, 2, 1):
        for rz in (0, 1):
            part = slot(0, sb).at[:, rz * D : rz * D + D]
            remote(part, part, b_s.at[sb - 1, rz], b_r.at[sb - 1, rz], twin).wait_recv()
        along_a(sb)
    own[2].wait()
    own[3].wait()
    for c in q_copies:
        c.wait_recv()

    def chunk(i, which):
        first = 2 * i
        return kv[pl.ds(first, 2), which].reshape(CHUNK, D)

    def stats(n, carry):
        i = STEPS - 1 - n
        for pos in range(len(ORDER)):
            if ORDER[pos][0]:
                @pl.when(i == pos // 2)
                def _(pos=pos):
                    part = kv.at[pos]
                    remote(part, part, a_s.at[pos], a_r.at[pos], twin).wait_recv()

        nq = q.shape[0]
        s = dot(chunk(i, 0), q[...], NT).reshape(CHUNK // 8, 8, nq)
        dp = dot(chunk(i, 1), g[...], NT).reshape(CHUNK // 8, 8, nq)
        before = top[...]
        peak = jnp.maximum(before, jnp.max(s, axis=0) * SCALE2)
        keep = jnp.exp2(before - peak)
        e = jnp.exp2(s * SCALE2 - peak[None])
        top[...] = peak
        mass[...] = mass[...] * keep + jnp.sum(e, axis=0)
        wsum[...] = wsum[...] * keep + jnp.sum(e * dp, axis=0)
        return carry

    lax.fori_loop(0, STEPS, stats, 0)
    peak = jnp.max(top[...], axis=0, keepdims=True)
    keep = jnp.exp2(top[...] - peak)
    total = jnp.sum(mass[...] * keep, axis=0, keepdims=True)
    weighted = jnp.sum(wsum[...] * keep, axis=0, keepdims=True)
    top[0:1] = peak + jnp.log2(total)
    wsum[0:1] = weighted / total

    def r1_copy(sa, sb):
        at = POS[BACK[sa], sb]
        return remote(
            out1.at[sa - 1, sb], in1.at[BACK[sa] - 1, sb],
            r1_s.at[POS[sa, sb]], r1_r.at[at], a_peer(GRAY[sa]),
        )

    def r1_sum(sb):
        for sa in (1, 2, 3):
            at = POS[sa, sb]
            remote(out1.at[sa - 1, sb], in1.at[sa - 1, sb], r1_s.at[at], r1_r.at[at], twin).wait_recv()
        acc[sb] += in1[0, sb].astype(F32) + in1[1, sb].astype(F32) + in1[2, sb].astype(F32)

    def r2_copy(s):
        return remote(
            acc.at[s], in2.at[BACK[s] - 1], r2_s.at[s - 1], r2_r.at[BACK[s] - 1], b_peer(GRAY[s])
        )

    def grads(i, carry):
        qq, gg = q[...], g[...]
        s = dot(chunk(i, 0), qq, NT)
        dp = dot(chunk(i, 1), gg, NT)
        p = jnp.exp2(s * SCALE2 - top[0:1])
        ds = (p * (dp - wsum[0:1])).astype(BF16)
        ds_all[i] = ds
        both = (dot(ds, qq, NN) * SCALE, dot(p.astype(BF16), gg, NN))
        for pos, (sa, sb) in enumerate(ORDER):
            @pl.when(i == pos // 2)
            def _(pos=pos, sa=sa, sb=sb):
                at = (pos % 2) * HALF
                for n in (0, 1):
                    part = both[n][at : at + HALF]
                    if sa:
                        out1[sa - 1, sb, n] = part.astype(BF16)
                    else:
                        acc[sb, n] = part
                if sa:
                    r1_copy(sa, sb).start()

        for at, slots in ((POS[0, 2] // 2, (1, 2)), (POS[0, 3] // 2, (3,))):
            @pl.when(i == at)
            def _(slots=slots):
                for sb in slots:
                    r1_sum(sb)
                    r2_copy(sb).start()

        return carry

    lax.fori_loop(0, STEPS, grads, 0)

    def make_dq(half):
        keys = kv[:, 0].reshape(STEPS * CHUNK, D)
        ds = ds_all[:, :, half * rows : half * rows + rows].reshape(STEPS * CHUNK, rows)
        dqs[half * rows : half * rows + rows] = dot(keys, ds, TN).T * SCALE

    make_dq(1)
    go(dqs.at[rows : 2 * rows], dq_out.at[:, mine], o_s.at[0], o_r.at[0], twin)
    r1_sum(0)
    for s in (1, 2, 3):
        remote(in2.at[s - 1], in2.at[s - 1], r2_s.at[s - 1], r2_r.at[s - 1], twin).wait_recv()
    fin[...] = acc[0] + in2[0] + in2[1] + in2[2]
    out3[...] = fin[...].astype(BF16)
    z_sums = [
        go(out3.at[:, at : at + D], in3.at[n], r3_s.at[n], r3_r.at[n], z_peers[n])
        for n, at in ((0, 0), (1, D), (2, D))
    ]
    make_dq(0)
    dq_here = pltpu.make_async_copy(dqs.at[0:rows], dq_out.at[:, mine], own_sem.at[0])
    dq_here.start()
    for c in z_sums:
        c.wait_recv()
    fin[:, 0:D] += in3[0].astype(F32) + in3[1].astype(F32) + in3[2].astype(F32)
    outs = [
        go(fin.at[n, 0:D], ref.at[:, mine], o_s.at[n + 1], o_r.at[n + 1], twin)
        for n, ref in enumerate((dk_out, dv_out))
    ]
    local = [
        pltpu.make_async_copy(fin.at[n, 0:D], ref.at[:, mine], own_sem.at[n + 1])
        for n, ref in enumerate((dk_out, dv_out))
    ]
    for c in local:
        c.start()
    for c in (dq_here, *local):
        c.wait()
    remote(dqs.at[0:rows], dq_out.at[:, other], o_s.at[0], o_r.at[0], twin).wait_recv()
    for n, ref in enumerate((dk_out, dv_out)):
        remote(fin.at[n, 0:D], ref.at[:, other], o_s.at[n + 1], o_r.at[n + 1], twin).wait_recv()
    for c in sends:
        c.wait_send()
    for s in (1, 2, 3):
        for sb in range(SIDE):
            r1_copy(s, sb).wait_send()
        r2_copy(s).wait_send()


def hand_over(dq, dk, dv, dq_out, dk_out, dv_out, sem):
    size = dq.shape[0] // PARTS
    pairs = [(dq.at[n * size : n * size + size], dq_out.at[n * size : n * size + size]) for n in range(PARTS)]
    pairs += [(dk, dk_out), (dv, dv_out)]
    copies = [pltpu.make_async_copy(src, dst, sem.at[n]) for n, (src, dst) in enumerate(pairs)]
    for c in copies:
        c.start()
    for c in copies:
        c.wait()


def local(queries, keys, values, dout):
    rows = queries.shape[0]
    key_rows = keys.shape[0]
    dma = pltpu.SemaphoreType.DMA
    vmem = pltpu.VMEM
    made = pl.pallas_call(
        kernel,
        out_shape=(
            jax.ShapeDtypeStruct((rows, 2 * D), F32),
            jax.ShapeDtypeStruct((key_rows, 2 * D), F32),
            jax.ShapeDtypeStruct((key_rows, 2 * D), F32),
        ),
        in_specs=[pl.BlockSpec(memory_space=pl.ANY)] * 4,
        out_specs=[pl.BlockSpec(memory_space=pl.ANY)] * 3,
        scratch_shapes=[
            vmem((2 * rows, D), BF16),
            vmem((2 * rows, D), BF16),
            vmem((2 * STEPS, 2, HALF, D), BF16),
            vmem((8, 2 * rows), F32),
            vmem((8, 2 * rows), F32),
            vmem((8, 2 * rows), F32),
            vmem((STEPS, CHUNK, 2 * rows), BF16),
            vmem((2 * rows, D), F32),
            vmem((3, SIDE, 2, HALF, D), BF16),
            vmem((3, SIDE, 2, HALF, D), BF16),
            vmem((SIDE, 2, HALF, D), F32),
            vmem((3, 2, HALF, D), F32),
            vmem((2, HALF, D), BF16),
            vmem((3, 2, D, D), BF16),
            vmem((2, HALF, D), F32),
            dma((4,)), dma((2,)), dma((2,)), dma, dma,
            dma((3, 2)), dma((3, 2)), dma((2 * STEPS,)), dma((2 * STEPS,)),
            dma((2 * STEPS,)), dma((2 * STEPS,)), dma((3,)), dma((3,)),
            dma((3,)), dma((3,)), dma((3,)), dma((3,)),
        ],
        compiler_params=pltpu.CompilerParams(
            collective_id=0, has_side_effects=True, vmem_limit_bytes=56 * 2**20
        ),
    )(queries, keys, values, dout)
    return pl.pallas_call(
        hand_over,
        out_shape=tuple(jax.ShapeDtypeStruct(m.shape, m.dtype) for m in made),
        in_specs=[pl.BlockSpec(memory_space=pl.ANY)] * 3,
        out_specs=[pl.BlockSpec(memory_space=pl.ANY)] * 3,
        scratch_shapes=[dma((PARTS + 2,))],
    )(*made)


def solution(mesh):
    return jax.shard_map(
        local,
        mesh=mesh,
        in_specs=(P(("pb", "kv"), None), P("kv", None), P("kv", None), P(("pb", "kv"), None)),
        out_specs=(P(("pb", "kv"), None), P("kv", None), P("kv", None)),
        check_vma=False,
    )
```

```python
import functools
import math

import jax
import jax.numpy as jnp
from jax import lax
from jax.experimental import pallas as pl
from jax.experimental.pallas import tpu as pltpu
from jax.sharding import PartitionSpec as P

D = 128
SIDE = 4
CHUNK = 512
HALF = 256
SCALE = 1.0 / math.sqrt(D)
SCALE2 = SCALE * math.log2(math.e)
GRAY = (0, 1, 3, 2)
BACK = (0, 2, 1, 3)
ORDER = (
    (3, 1), (1, 1), (2, 1), (3, 2), (3, 3), (1, 3), (1, 2), (2, 2),
    (2, 3), (3, 0), (0, 1), (0, 2), (0, 3), (1, 0), (2, 0), (0, 0),
)
POS = {piece: n for n, piece in enumerate(ORDER)}
STEPS = len(ORDER) // 2
LATER = 6
BY_Z = ((3, 3), (2, 1), (3, 2), (3, 1), (1, 1))
Z_STEP = 3
BY_A = ((2, 3), (1, 3), (1, 2), (2, 2))
NT = (((1,), (1,)), ((), ()))
NN = (((1,), (0,)), ((), ()))
TN = (((0,), (0,)), ((), ()))
F32 = jnp.float32
BF16 = jnp.bfloat16


def dot(a, b, dims):
    return lax.dot_general(a, b, dims, preferred_element_type=F32)


def remote(src, dst, send, recv, device):
    return pltpu.make_async_remote_copy(
        src_ref=src, dst_ref=dst, send_sem=send, recv_sem=recv,
        device_id=device, device_id_type=pl.DeviceIdType.MESH,
    )


def kernel(
    q_in, k_in, v_in, g_in, dq_out, dk_out, dv_out,
    q, g, kv, top, mass, wsum, e_all, tops, ds_all, dqt, dqs, out1, in1, acc, in2, out3, in3, fin,
    own_sem, q_s, q_r, k_s, k_r, z_s, z_r,
    r1_s, r1_r, r2_s, r2_r, r3_s, r3_r, o_s, o_r,
):
    rows = q_in.shape[0]
    pb, kvi = lax.axis_index("pb"), lax.axis_index("kv")
    core, zh = pb % 2, pb // 2
    y, x, zl = kvi // 8, (kvi // 2) % 4, kvi % 2

    def a_peer(d):
        return (pb, (((y + d * (1 - core)) % SIDE) * SIDE + (x + d * core) % SIDE) * 2 + zl)

    def b_peer(d):
        return (pb, (((y + d * core) % SIDE) * SIDE + (x + d * (1 - core)) % SIDE) * 2 + zl)

    twin = (zh * 2 + 1 - core, kvi)
    far_z = (1 - zh) * 2 + core
    near = kvi + 1 - 2 * zl
    z_peer = (pb, near)
    z_peers = ((far_z, kvi), z_peer, (far_z, near))
    mine = pl.ds(pl.multiple_of(core * D, D), D)
    other = pl.ds(pl.multiple_of((1 - core) * D, D), D)

    def slot(sa, sb):
        return kv.at[POS[sa, sb]]

    barrier = pltpu.get_barrier_semaphore()
    peers = [twin, *z_peers]
    peers += [a_peer(d) for d in (1, 2, 3)] + [b_peer(d) for d in (1, 2, 3)]
    for peer in peers:
        pl.semaphore_signal(barrier, inc=1, device_id=peer, device_id_type=pl.DeviceIdType.MESH)

    here = slot(0, 0)
    own = []
    for n, (src, dst) in enumerate((
        (k_in.at[:, mine], here.at[0, 0:D]),
        (v_in.at[:, mine], here.at[1, 0:D]),
        (q_in.at[:, mine], q.at[0:rows]),
        (g_in.at[:, mine], g.at[0:rows]),
    )):
        own.append(pltpu.make_async_copy(src, dst, own_sem.at[n]))
        own[-1].start()
    pl.semaphore_wait(barrier, len(peers))

    sends = []

    def go(*args):
        c = remote(*args)
        c.start()
        sends.append(c)
        return c

    own[0].wait()
    own[1].wait()

    def part(pos, half):
        return kv.at[pos, :, half * D : half * D + D]

    def along_b(s, half):
        at = POS[0, BACK[s]]
        go(
            part(POS[0, 0], half), part(at, half),
            k_s.at[POS[0, s], half], k_r.at[at, half], b_peer(GRAY[s]),
        )

    def a_copy(sa, sb, half):
        at = POS[BACK[sa], sb]
        return (
            part(POS[0, sb], half), part(at, half),
            k_s.at[POS[sa, sb], half], k_r.at[at, half], a_peer(GRAY[sa]),
        )

    def along_a(sa, sb, half):
        go(*a_copy(sa, sb, half))

    def z_copy(pos, n):
        return remote(
            kv.at[pos, n, 0:D], kv.at[pos, n, D:HALF], z_s.at[pos, n], z_r.at[pos, n], z_peers[1 + n]
        )

    def along_z(pos):
        for n in (0, 1):
            z_copy(pos, n).start()

    def have(pos, half):
        remote(
            part(pos, half), part(pos, half), k_s.at[pos, half], k_r.at[pos, half], twin
        ).wait_recv()

    def have_z(pos):
        for n in (0, 1):
            z_copy(pos, n).wait_recv()

    for s in (3, 1, 2):
        along_b(s, 0)
    for sa in (3, 1, 2):
        along_a(sa, 0, 0)
    along_z(POS[0, 0])
    q_copies = [
        go(q_in.at[:, other], q.at[rows : 2 * rows], q_s.at[0], q_r.at[0], twin),
        go(g_in.at[:, other], g.at[rows : 2 * rows], q_s.at[1], q_r.at[1], twin),
    ]
    top[...] = jnp.full_like(top, -1e30)
    mass[...] = jnp.zeros_like(mass)
    wsum[...] = jnp.zeros_like(wsum)
    have_z(POS[0, 0])
    for s in (3, 1, 2):
        along_b(s, 1)
    for sa in (2, 1, 3):
        along_a(sa, 0, 1)
    for sb in (3, 1, 2):
        have(POS[0, sb], 0)
        for sa in (3, 2, 1):
            along_a(sa, sb, 0)
    own[2].wait()
    own[3].wait()
    for c in q_copies:
        c.wait_recv()

    def chunk(i, which):
        first = 2 * i
        return kv[pl.ds(first, 2), which].reshape(CHUNK, D)

    def stats(n, carry):
        i = STEPS - 1 - n
        for step in range(STEPS):
            @pl.when(n == step)
            def _(step=step):
                if step == 0:
                    have(POS[0, 2], 1)
                    have(POS[0, 3], 1)
                    for sa, sb in BY_A:
                        remote(*a_copy(sa, sb, 1)).start()
                if step == Z_STEP:
                    for piece in BY_Z:
                        have(POS[piece], 0)
                        along_z(POS[piece])
                for pos in (2 * (STEPS - 1 - step) + 1, 2 * (STEPS - 1 - step)):
                    sa, sb = ORDER[pos]
                    if (sa, sb) in BY_Z:
                        have_z(pos)
                        continue
                    if sa:
                        have(pos, 0)
                    if (sa, sb) not in ((0, 0), (0, 2), (0, 3)):
                        have(pos, 1)

        nq = q.shape[0]
        s = dot(chunk(i, 0), q[...], NT).reshape(CHUNK // 8, 8, nq)
        dp = dot(chunk(i, 1), g[...], NT).reshape(CHUNK // 8, 8, nq)
        before = top[...]
        peak = jnp.maximum(before, jnp.max(s, axis=0) * SCALE2)
        keep = jnp.exp2(before - peak)
        e = jnp.exp2(s * SCALE2 - peak[None])
        top[...] = peak
        e_all[i] = e.reshape(CHUNK, nq)
        tops[i] = peak
        mass[...] = mass[...] * keep + jnp.sum(e, axis=0)
        wsum[...] = wsum[...] * keep + jnp.sum(e * dp, axis=0)
        return carry

    lax.fori_loop(0, STEPS, stats, 0)
    peak = jnp.max(top[...], axis=0, keepdims=True)
    keep = jnp.exp2(top[...] - peak)
    total = jnp.sum(mass[...] * keep, axis=0, keepdims=True)
    weighted = jnp.sum(wsum[...] * keep, axis=0, keepdims=True)
    top[0:1] = peak + jnp.log2(total)
    wsum[0:1] = weighted / total

    def r1_copy(sa, sb):
        at = POS[BACK[sa], sb]
        return remote(
            out1.at[sa - 1, sb], in1.at[BACK[sa] - 1, sb],
            r1_s.at[POS[sa, sb]], r1_r.at[at], a_peer(GRAY[sa]),
        )

    def r1_sum(sb):
        for sa in (1, 2, 3):
            at = POS[sa, sb]
            remote(out1.at[sa - 1, sb], in1.at[sa - 1, sb], r1_s.at[at], r1_r.at[at], twin).wait_recv()
        acc[sb] += in1[0, sb].astype(F32) + in1[1, sb].astype(F32) + in1[2, sb].astype(F32)

    def r2_copy(s):
        return remote(
            acc.at[s], in2.at[BACK[s] - 1], r2_s.at[s - 1], r2_r.at[BACK[s] - 1], b_peer(GRAY[s])
        )

    def key_grads(i, at, size, later):
        nq = q.shape[0]
        qq, gg = q[...], g[...]
        if size == CHUNK:
            kc, vc = chunk(i, 0), chunk(i, 1)
        else:
            kc, vc = kv[2 * i + at // HALF, 0], kv[2 * i + at // HALF, 1]
        dp = dot(vc, gg, NT)
        factor = jnp.exp2(tops[i] - top[0:1])
        e = e_all[i, at : at + size].reshape(size // 8, 8, nq)
        p = (e * factor[None]).reshape(size, nq)
        ds = (p * (dp - wsum[0:1])).astype(BF16)
        if later:
            ds_all[i - LATER, at : at + size] = ds
        else:
            dqt[...] += dot(kc, ds, TN)
        return dot(ds, qq, NN) * SCALE, dot(p.astype(BF16), gg, NN)

    def place(sa, sb, both, at):
        for n in (0, 1):
            part = both[n][at : at + HALF]
            if sa:
                out1[sa - 1, sb, n] = part.astype(BF16)
            else:
                acc[sb, n] = part
        if sa:
            r1_copy(sa, sb).start()

    def grads(later, i, carry):
        both = key_grads(i, 0, CHUNK, later)
        for pos, (sa, sb) in enumerate(ORDER[:-2]):
            @pl.when(i == pos // 2)
            def _(pos=pos, sa=sa, sb=sb):
                place(sa, sb, both, (pos % 2) * HALF)

        for at, slots in ((POS[0, 2] // 2, (1, 2)), (POS[0, 3] // 2, (3,))):
            @pl.when(i == at)
            def _(slots=slots):
                for sb in slots:
                    r1_sum(sb)
                    r2_copy(sb).start()

        return carry

    dqt[...] = jnp.zeros_like(dqt)
    lax.fori_loop(0, LATER, functools.partial(grads, False), 0)
    lax.fori_loop(LATER, STEPS - 1, functools.partial(grads, True), 0)
    for n, (sa, sb) in enumerate(ORDER[-2:]):
        place(sa, sb, key_grads(STEPS - 1, n * HALF, HALF, True), 0)

    def make_dq(half):
        size = (STEPS - LATER) * CHUNK
        queries = slice(half * rows, half * rows + rows)
        keys = kv[2 * LATER :, 0].reshape(size, D)
        ds = ds_all[:, :, queries].reshape(size, rows)
        dqs[queries] = (dqt[:, queries] + dot(keys, ds, TN)).T * SCALE

    make_dq(1)
    go(dqs.at[rows : 2 * rows], dq_out.at[:, mine], o_s.at[0], o_r.at[0], twin)
    r1_sum(0)
    for s in (1, 2, 3):
        remote(in2.at[s - 1], in2.at[s - 1], r2_s.at[s - 1], r2_r.at[s - 1], twin).wait_recv()
    fin[...] = acc[0] + in2[0] + in2[1] + in2[2]
    out3[...] = fin[...].astype(BF16)
    z_sums = [
        go(out3.at[:, at : at + D], in3.at[n], r3_s.at[n], r3_r.at[n], z_peers[n])
        for n, at in ((0, 0), (1, D), (2, D))
    ]
    make_dq(0)
    dq_here = pltpu.make_async_copy(dqs.at[0:rows], dq_out.at[:, mine], own_sem.at[0])
    dq_here.start()
    for c in z_sums:
        c.wait_recv()
    fin[:, 0:D] += in3[0].astype(F32) + in3[1].astype(F32) + in3[2].astype(F32)
    outs = [
        go(fin.at[n, 0:D], ref.at[:, mine], o_s.at[n + 1], o_r.at[n + 1], twin)
        for n, ref in enumerate((dk_out, dv_out))
    ]
    local = [
        pltpu.make_async_copy(fin.at[n, 0:D], ref.at[:, mine], own_sem.at[n + 1])
        for n, ref in enumerate((dk_out, dv_out))
    ]
    for c in local:
        c.start()
    for c in (dq_here, *local):
        c.wait()
    remote(dqs.at[0:rows], dq_out.at[:, other], o_s.at[0], o_r.at[0], twin).wait_recv()
    for n, ref in enumerate((dk_out, dv_out)):
        remote(fin.at[n, 0:D], ref.at[:, other], o_s.at[n + 1], o_r.at[n + 1], twin).wait_recv()
    for c in sends:
        c.wait_send()
    for sa, sb in BY_A:
        remote(*a_copy(sa, sb, 1)).wait_send()
    for piece in ((0, 0), *BY_Z):
        for n in (0, 1):
            z_copy(POS[piece], n).wait_send()
    for s in (1, 2, 3):
        for sb in range(SIDE):
            r1_copy(s, sb).wait_send()
        r2_copy(s).wait_send()


def hand_over(dq, dk, dv, dq_out, dk_out, dv_out, held, sem_in, sem_out):
    size = held.shape[1]
    places = [(src, dst, 0) for src, dst in ((dk, dk_out), (dv, dv_out))]
    places += [(dq, dq_out, at) for at in range(0, dq.shape[0], size)]
    ins, outs = [], []
    for n, (src, dst, at) in enumerate(places):
        ins.append(pltpu.make_async_copy(src.at[at : at + size], held.at[n], sem_in.at[n]))
        outs.append(pltpu.make_async_copy(held.at[n], dst.at[at : at + size], sem_out.at[n]))
        ins[-1].start()
    for here, there in zip(ins, outs):
        here.wait()
        there.start()
    for there in outs:
        there.wait()


def local(queries, keys, values, dout):
    rows = queries.shape[0]
    key_rows = keys.shape[0]
    dma = pltpu.SemaphoreType.DMA
    vmem = pltpu.VMEM
    blocks = 2 + rows // key_rows
    made = pl.pallas_call(
        kernel,
        out_shape=(
            jax.ShapeDtypeStruct((rows, 2 * D), F32),
            jax.ShapeDtypeStruct((key_rows, 2 * D), F32),
            jax.ShapeDtypeStruct((key_rows, 2 * D), F32),
        ),
        in_specs=[pl.BlockSpec(memory_space=pl.ANY)] * 4,
        out_specs=[pl.BlockSpec(memory_space=pl.ANY)] * 3,
        scratch_shapes=[
            vmem((2 * rows, D), BF16),
            vmem((2 * rows, D), BF16),
            vmem((2 * STEPS, 2, HALF, D), BF16),
            vmem((8, 2 * rows), F32),
            vmem((8, 2 * rows), F32),
            vmem((8, 2 * rows), F32),
            vmem((STEPS, CHUNK, 2 * rows), F32),
            vmem((STEPS, 8, 2 * rows), F32),
            vmem((STEPS - LATER, CHUNK, 2 * rows), BF16),
            vmem((D, 2 * rows), F32),
            vmem((2 * rows, D), F32),
            vmem((3, SIDE, 2, HALF, D), BF16),
            vmem((3, SIDE, 2, HALF, D), BF16),
            vmem((SIDE, 2, HALF, D), F32),
            vmem((3, 2, HALF, D), F32),
            vmem((2, HALF, D), BF16),
            vmem((3, 2, D, D), BF16),
            vmem((2, HALF, D), F32),
            dma((4,)), dma((2,)), dma((2,)),
            dma((2 * STEPS, 2)), dma((2 * STEPS, 2)), dma((2 * STEPS, 2)), dma((2 * STEPS, 2)),
            dma((2 * STEPS,)), dma((2 * STEPS,)), dma((3,)), dma((3,)),
            dma((3,)), dma((3,)), dma((3,)), dma((3,)),
        ],
        compiler_params=pltpu.CompilerParams(
            collective_id=0, has_side_effects=True, vmem_limit_bytes=60 * 2**20
        ),
    )(queries, keys, values, dout)
    return pl.pallas_call(
        hand_over,
        out_shape=tuple(jax.ShapeDtypeStruct(m.shape, m.dtype) for m in made),
        in_specs=[pl.BlockSpec(memory_space=pl.ANY)] * 3,
        out_specs=[pl.BlockSpec(memory_space=pl.ANY)] * 3,
        scratch_shapes=[vmem((blocks, key_rows, 2 * D), F32), dma((blocks,)), dma((blocks,))],
    )(*made)


def solution(mesh):
    return jax.shard_map(
        local,
        mesh=mesh,
        in_specs=(P(("pb", "kv"), None), P("kv", None), P("kv", None), P(("pb", "kv"), None)),
        out_specs=(P(("pb", "kv"), None), P("kv", None), P("kv", None)),
        check_vma=False,
    )
```

```python
import functools
import math

import jax
import jax.numpy as jnp
from jax import lax
from jax.experimental import pallas as pl
from jax.experimental.pallas import tpu as pltpu
from jax.sharding import PartitionSpec as P

D = 128
SIDE = 4
CHUNK = 512
HALF = 256
SCALE = 1.0 / math.sqrt(D)
SCALE2 = SCALE * math.log2(math.e)
GRAY = (0, 1, 3, 2)
BACK = (0, 2, 1, 3)
ORDER = (
    (3, 1), (1, 1), (2, 1), (3, 2), (3, 3), (1, 3), (1, 2), (2, 2),
    (2, 3), (3, 0), (0, 1), (0, 2), (0, 3), (1, 0), (2, 0), (0, 0),
)
POS = {piece: n for n, piece in enumerate(ORDER)}
STEPS = len(ORDER) // 2
LATER = 6
BY_Z = ((3, 1), (1, 1), (2, 1), (3, 2))
BY_A = ((3, 3), (1, 3), (2, 3), (1, 2), (2, 2))
SCHEDULE = (
    ((0, 0, 0), (0, 3, 0), (0, 1, 0), (0, 2, 0)),
    ((0, 0, 1), (1, 0, 0), (2, 0, 0), (3, 0, 0)),
    ((0, 3, 1), (0, 1, 1), (0, 2, 1), (1, 0, 1)),
    ((2, 0, 1), (3, 0, 1), (2, 3, 0), (3, 3, 0)),
    ((1, 3, 0), (1, 1, 0), (2, 1, 0), (3, 1, 0)),
    ((1, 2, 0), (2, 2, 0), (3, 2, 0), (3, 3, 1)),
    ((1, 3, 1), (2, 3, 1), (1, 2, 1), (2, 2, 1)),
    ((3, 1, 1), (1, 1, 1), (2, 1, 1), (3, 2, 1)),
)
A_STEP = 2
Z_STEPS = {4: BY_Z[:3], 5: BY_Z[3:]}
NT = (((1,), (1,)), ((), ()))
NN = (((1,), (0,)), ((), ()))
TN = (((0,), (0,)), ((), ()))
F32 = jnp.float32
BF16 = jnp.bfloat16


def dot(a, b, dims):
    return lax.dot_general(a, b, dims, preferred_element_type=F32)


def remote(src, dst, send, recv, device):
    return pltpu.make_async_remote_copy(
        src_ref=src, dst_ref=dst, send_sem=send, recv_sem=recv,
        device_id=device, device_id_type=pl.DeviceIdType.MESH,
    )


def kernel(
    q_in, k_in, v_in, g_in, dq_out, dk_out, dv_out,
    q, g, kv, top, mass, wsum, e_all, tops, ds_all, dqt, dqs, out1, in1, acc, in2, out3, in3, fin,
    own_sem, q_s, q_r, k_s, k_r, z_s, z_r,
    r1_s, r1_r, r2_s, r2_r, r3_s, r3_r, o_s, o_r,
):
    rows = q_in.shape[0]
    pb, kvi = lax.axis_index("pb"), lax.axis_index("kv")
    core, zh = pb % 2, pb // 2
    y, x, zl = kvi // 8, (kvi // 2) % 4, kvi % 2

    def a_peer(d):
        return (pb, (((y + d * (1 - core)) % SIDE) * SIDE + (x + d * core) % SIDE) * 2 + zl)

    def b_peer(d):
        return (pb, (((y + d * core) % SIDE) * SIDE + (x + d * (1 - core)) % SIDE) * 2 + zl)

    twin = (zh * 2 + 1 - core, kvi)
    far_z = (1 - zh) * 2 + core
    near = kvi + 1 - 2 * zl
    z_peer = (pb, near)
    z_peers = ((far_z, kvi), z_peer, (far_z, near))
    mine = pl.ds(pl.multiple_of(core * D, D), D)
    other = pl.ds(pl.multiple_of((1 - core) * D, D), D)

    def slot(sa, sb):
        return kv.at[POS[sa, sb]]

    barrier = pltpu.get_barrier_semaphore()
    peers = [twin, *z_peers]
    peers += [a_peer(d) for d in (1, 2, 3)] + [b_peer(d) for d in (1, 2, 3)]
    for peer in peers:
        pl.semaphore_signal(barrier, inc=1, device_id=peer, device_id_type=pl.DeviceIdType.MESH)

    here = slot(0, 0)
    own = []
    for n, (src, dst) in enumerate((
        (k_in.at[:, mine], here.at[0, 0:D]),
        (v_in.at[:, mine], here.at[1, 0:D]),
        (q_in.at[:, mine], q.at[0:rows]),
        (g_in.at[:, mine], g.at[0:rows]),
    )):
        own.append(pltpu.make_async_copy(src, dst, own_sem.at[n]))
        own[-1].start()
    pl.semaphore_wait(barrier, len(peers))

    sends = []

    def go(*args):
        c = remote(*args)
        c.start()
        sends.append(c)
        return c

    own[0].wait()
    own[1].wait()

    def part(pos, half):
        return kv.at[pos, :, half * D : half * D + D]

    def along_b(s, half):
        at = POS[0, BACK[s]]
        go(
            part(POS[0, 0], half), part(at, half),
            k_s.at[POS[0, s], half], k_r.at[at, half], b_peer(GRAY[s]),
        )

    def along_a(sa, sb, half):
        at = POS[BACK[sa], sb]
        go(
            part(POS[0, sb], half), part(at, half),
            k_s.at[POS[sa, sb], half], k_r.at[at, half], a_peer(GRAY[sa]),
        )

    def z_copy(pos, n):
        return remote(
            kv.at[pos, n, 0:D], kv.at[pos, n, D:HALF], z_s.at[pos, n], z_r.at[pos, n], z_peers[1 + n]
        )

    def along_z(pos):
        for n in (0, 1):
            c = z_copy(pos, n)
            c.start()
            sends.append(c)

    def have(pos, half):
        remote(
            part(pos, half), part(pos, half), k_s.at[pos, half], k_r.at[pos, half], twin
        ).wait_recv()

    def have_z(pos):
        for n in (0, 1):
            z_copy(pos, n).wait_recv()

    for s in (3, 1, 2):
        along_b(s, 0)
    for sa in (3, 1, 2):
        along_a(sa, 0, 0)
    along_z(POS[0, 0])
    q_copies = [
        go(q_in.at[:, other], q.at[rows : 2 * rows], q_s.at[0], q_r.at[0], twin),
        go(g_in.at[:, other], g.at[rows : 2 * rows], q_s.at[1], q_r.at[1], twin),
    ]
    top[...] = jnp.full_like(top, -1e30)
    mass[...] = jnp.zeros_like(mass)
    wsum[...] = jnp.zeros_like(wsum)
    waited = {(0, 0, 0)}

    def need(sa, sb, half):
        if (sa, sb, half) in waited:
            return
        waited.add((sa, sb, half))
        if half and (sa, sb) in ((0, 0), *BY_Z):
            have_z(POS[sa, sb])
        else:
            have(POS[sa, sb], half)

    need(0, 0, 1)
    for s in (3, 1, 2):
        along_b(s, 1)
    for sa in (1, 2, 3):
        along_a(sa, 0, 1)
    for sb in (3, 1, 2):
        need(0, sb, 0)
        for sa in (3, 2, 1):
            along_a(sa, sb, 0)
    own[2].wait()
    own[3].wait()
    for c in q_copies:
        c.wait_recv()

    def chunk(i, which):
        first = 2 * i
        return kv[pl.ds(first, 2), which].reshape(CHUNK, D)

    def stats(halves):
        nq = q.shape[0]
        kc, vc = (
            jnp.concatenate([kv[POS[sa, sb], n, h * D : h * D + D] for sa, sb, h in halves])
            for n in (0, 1)
        )
        s = dot(kc, q[...], NT).reshape(CHUNK // 8, 8, nq)
        dp = dot(vc, g[...], NT).reshape(CHUNK // 8, 8, nq)
        before = top[...]
        peak = jnp.maximum(before, jnp.max(s, axis=0) * SCALE2)
        keep = jnp.exp2(before - peak)
        e = jnp.exp2(s * SCALE2 - peak[None])
        top[...] = peak
        for n, (sa, sb, h) in enumerate(halves):
            e_all[POS[sa, sb], h] = e[n * 16 : n * 16 + 16].reshape(D, nq)
            tops[POS[sa, sb], h] = peak
        mass[...] = mass[...] * keep + jnp.sum(e, axis=0)
        wsum[...] = wsum[...] * keep + jnp.sum(e * dp, axis=0)

    for step, halves in enumerate(SCHEDULE):
        if step == A_STEP:
            for sa, sb in BY_A:
                need(0, sb, 1)
                along_a(sa, sb, 1)
        for sa, sb in Z_STEPS.get(step, ()):
            need(sa, sb, 0)
            along_z(POS[sa, sb])
        for sa, sb, half in halves:
            need(sa, sb, half)
        stats(halves)
    peak = jnp.max(top[...], axis=0, keepdims=True)
    keep = jnp.exp2(top[...] - peak)
    total = jnp.sum(mass[...] * keep, axis=0, keepdims=True)
    weighted = jnp.sum(wsum[...] * keep, axis=0, keepdims=True)
    top[0:1] = peak + jnp.log2(total)
    wsum[0:1] = weighted / total

    def r1_copy(sa, sb):
        at = POS[BACK[sa], sb]
        return remote(
            out1.at[sa - 1, sb], in1.at[BACK[sa] - 1, sb],
            r1_s.at[POS[sa, sb]], r1_r.at[at], a_peer(GRAY[sa]),
        )

    def r1_sum(sb):
        for sa in (1, 2, 3):
            at = POS[sa, sb]
            remote(out1.at[sa - 1, sb], in1.at[sa - 1, sb], r1_s.at[at], r1_r.at[at], twin).wait_recv()
        acc[sb] += in1[0, sb].astype(F32) + in1[1, sb].astype(F32) + in1[2, sb].astype(F32)

    def r2_copy(s):
        return remote(
            acc.at[s], in2.at[BACK[s] - 1], r2_s.at[s - 1], r2_r.at[BACK[s] - 1], b_peer(GRAY[s])
        )

    def key_grads(i, at, size, later):
        nq = q.shape[0]
        qq, gg = q[...], g[...]
        if size == CHUNK:
            kc, vc = chunk(i, 0), chunk(i, 1)
        else:
            kc, vc = kv[2 * i + at // HALF, 0], kv[2 * i + at // HALF, 1]
        pieces = pl.ds(2 * i + at // HALF, size // HALF)
        halves = size // D
        dp = dot(vc, gg, NT)
        factor = jnp.exp2(tops[pieces].reshape(halves, 1, 8, nq) - top[0:1])
        e = e_all[pieces].reshape(halves, D // 8, 8, nq)
        p = (e * factor).reshape(size, nq)
        ds = (p * (dp - wsum[0:1])).astype(BF16)
        if later:
            ds_all[i - LATER, at : at + size] = ds
        else:
            dqt[...] += dot(kc, ds, TN)
        return dot(ds, qq, NN) * SCALE, dot(p.astype(BF16), gg, NN)

    def place(sa, sb, both, at):
        for n in (0, 1):
            part = both[n][at : at + HALF]
            if sa:
                out1[sa - 1, sb, n] = part.astype(BF16)
            else:
                acc[sb, n] = part
        if sa:
            r1_copy(sa, sb).start()

    def grads(later, i, carry):
        both = key_grads(i, 0, CHUNK, later)
        for pos, (sa, sb) in enumerate(ORDER[:-2]):
            @pl.when(i == pos // 2)
            def _(pos=pos, sa=sa, sb=sb):
                place(sa, sb, both, (pos % 2) * HALF)

        for at, slots in ((POS[0, 2] // 2, (1, 2)), (POS[0, 3] // 2, (3,))):
            @pl.when(i == at)
            def _(slots=slots):
                for sb in slots:
                    r1_sum(sb)
                    r2_copy(sb).start()

        return carry

    dqt[...] = jnp.zeros_like(dqt)
    lax.fori_loop(0, LATER, functools.partial(grads, False), 0)
    lax.fori_loop(LATER, STEPS - 1, functools.partial(grads, True), 0)
    for n, (sa, sb) in enumerate(ORDER[-2:]):
        place(sa, sb, key_grads(STEPS - 1, n * HALF, HALF, True), 0)

    def make_dq(half):
        size = (STEPS - LATER) * CHUNK
        queries = slice(half * rows, half * rows + rows)
        keys = kv[2 * LATER :, 0].reshape(size, D)
        ds = ds_all[:, :, queries].reshape(size, rows)
        dqs[queries] = (dqt[:, queries] + dot(keys, ds, TN)).T * SCALE

    make_dq(1)
    go(dqs.at[rows : 2 * rows], dq_out.at[:, mine], o_s.at[0], o_r.at[0], twin)
    r1_sum(0)
    for s in (1, 2, 3):
        remote(in2.at[s - 1], in2.at[s - 1], r2_s.at[s - 1], r2_r.at[s - 1], twin).wait_recv()
    fin[...] = acc[0] + in2[0] + in2[1] + in2[2]
    out3[...] = fin[...].astype(BF16)
    z_sums = [
        go(out3.at[:, at : at + D], in3.at[n], r3_s.at[n], r3_r.at[n], z_peers[n])
        for n, at in ((0, 0), (1, D), (2, D))
    ]
    make_dq(0)
    dq_here = pltpu.make_async_copy(dqs.at[0:rows], dq_out.at[:, mine], own_sem.at[0])
    dq_here.start()
    for c in z_sums:
        c.wait_recv()
    fin[:, 0:D] += in3[0].astype(F32) + in3[1].astype(F32) + in3[2].astype(F32)
    outs = [
        go(fin.at[n, 0:D], ref.at[:, mine], o_s.at[n + 1], o_r.at[n + 1], twin)
        for n, ref in enumerate((dk_out, dv_out))
    ]
    local = [
        pltpu.make_async_copy(fin.at[n, 0:D], ref.at[:, mine], own_sem.at[n + 1])
        for n, ref in enumerate((dk_out, dv_out))
    ]
    for c in local:
        c.start()
    for c in (dq_here, *local):
        c.wait()
    remote(dqs.at[0:rows], dq_out.at[:, other], o_s.at[0], o_r.at[0], twin).wait_recv()
    for n, ref in enumerate((dk_out, dv_out)):
        remote(fin.at[n, 0:D], ref.at[:, other], o_s.at[n + 1], o_r.at[n + 1], twin).wait_recv()
    for c in sends:
        c.wait_send()
    for s in (1, 2, 3):
        for sb in range(SIDE):
            r1_copy(s, sb).wait_send()
        r2_copy(s).wait_send()


def hand_over(dq, dk, dv, dq_out, dk_out, dv_out, held, sem_in, sem_out):
    size = held.shape[1]
    places = [(src, dst, 0) for src, dst in ((dk, dk_out), (dv, dv_out))]
    places += [(dq, dq_out, at) for at in range(0, dq.shape[0], size)]
    ins, outs = [], []
    for n, (src, dst, at) in enumerate(places):
        ins.append(pltpu.make_async_copy(src.at[at : at + size], held.at[n], sem_in.at[n]))
        outs.append(pltpu.make_async_copy(held.at[n], dst.at[at : at + size], sem_out.at[n]))
        ins[-1].start()
    for here, there in zip(ins, outs):
        here.wait()
        there.start()
    for there in outs:
        there.wait()


def local(queries, keys, values, dout):
    rows = queries.shape[0]
    key_rows = keys.shape[0]
    dma = pltpu.SemaphoreType.DMA
    vmem = pltpu.VMEM
    blocks = 2 + rows // key_rows
    made = pl.pallas_call(
        kernel,
        out_shape=(
            jax.ShapeDtypeStruct((rows, 2 * D), F32),
            jax.ShapeDtypeStruct((key_rows, 2 * D), F32),
            jax.ShapeDtypeStruct((key_rows, 2 * D), F32),
        ),
        in_specs=[pl.BlockSpec(memory_space=pl.ANY)] * 4,
        out_specs=[pl.BlockSpec(memory_space=pl.ANY)] * 3,
        scratch_shapes=[
            vmem((2 * rows, D), BF16),
            vmem((2 * rows, D), BF16),
            vmem((2 * STEPS, 2, HALF, D), BF16),
            vmem((8, 2 * rows), F32),
            vmem((8, 2 * rows), F32),
            vmem((8, 2 * rows), F32),
            vmem((2 * STEPS, 2, D, 2 * rows), F32),
            vmem((2 * STEPS, 2, 8, 2 * rows), F32),
            vmem((STEPS - LATER, CHUNK, 2 * rows), BF16),
            vmem((D, 2 * rows), F32),
            vmem((2 * rows, D), F32),
            vmem((3, SIDE, 2, HALF, D), BF16),
            vmem((3, SIDE, 2, HALF, D), BF16),
            vmem((SIDE, 2, HALF, D), F32),
            vmem((3, 2, HALF, D), F32),
            vmem((2, HALF, D), BF16),
            vmem((3, 2, D, D), BF16),
            vmem((2, HALF, D), F32),
            dma((4,)), dma((2,)), dma((2,)),
            dma((2 * STEPS, 2)), dma((2 * STEPS, 2)), dma((2 * STEPS, 2)), dma((2 * STEPS, 2)),
            dma((2 * STEPS,)), dma((2 * STEPS,)), dma((3,)), dma((3,)),
            dma((3,)), dma((3,)), dma((3,)), dma((3,)),
        ],
        compiler_params=pltpu.CompilerParams(
            collective_id=0, has_side_effects=True, vmem_limit_bytes=60 * 2**20
        ),
    )(queries, keys, values, dout)
    return pl.pallas_call(
        hand_over,
        out_shape=tuple(jax.ShapeDtypeStruct(m.shape, m.dtype) for m in made),
        in_specs=[pl.BlockSpec(memory_space=pl.ANY)] * 3,
        out_specs=[pl.BlockSpec(memory_space=pl.ANY)] * 3,
        scratch_shapes=[vmem((blocks, key_rows, 2 * D), F32), dma((blocks,)), dma((blocks,))],
    )(*made)


def solution(mesh):
    return jax.shard_map(
        local,
        mesh=mesh,
        in_specs=(P(("pb", "kv"), None), P("kv", None), P("kv", None), P(("pb", "kv"), None)),
        out_specs=(P(("pb", "kv"), None), P("kv", None), P("kv", None)),
        check_vma=False,
    )
```

```python
import functools
import math

import jax
import jax.numpy as jnp
from jax import lax
from jax.experimental import pallas as pl
from jax.experimental.pallas import tpu as pltpu
from jax.sharding import PartitionSpec as P

D = 128
SIDE = 4
CHUNK = 512
HALF = 256
SCALE = 1.0 / math.sqrt(D)
SCALE2 = SCALE * math.log2(math.e)
GRAY = (0, 1, 3, 2)
BACK = (0, 2, 1, 3)
ORDER = (
    (3, 1), (1, 1), (2, 1), (3, 2), (3, 3), (1, 3), (1, 2), (2, 2),
    (2, 3), (3, 0), (0, 1), (0, 2), (0, 3), (1, 0), (2, 0), (0, 0),
)
POS = {piece: n for n, piece in enumerate(ORDER)}
STEPS = len(ORDER) // 2
LATER = STEPS - 1
BY_Z = ((3, 1), (1, 1), (2, 1), (3, 2))
BY_A = ((3, 3), (1, 3), (2, 3), (1, 2), (2, 2))
SCHEDULE = (
    ((0, 0, 0), (0, 3, 0), (0, 1, 0), (0, 2, 0)),
    ((0, 0, 1), (1, 0, 0), (2, 0, 0), (3, 0, 0)),
    ((0, 3, 1), (0, 1, 1), (0, 2, 1), (1, 0, 1)),
    ((2, 0, 1), (3, 0, 1), (2, 3, 0), (3, 3, 0)),
    ((1, 3, 0), (1, 1, 0), (2, 1, 0), (3, 1, 0)),
    ((1, 2, 0), (2, 2, 0), (3, 2, 0), (3, 3, 1)),
    ((1, 3, 1), (2, 3, 1), (1, 2, 1), (2, 2, 1)),
    ((3, 1, 1), (1, 1, 1), (2, 1, 1), (3, 2, 1)),
)
A_STEP = 2
Z_STEPS = {4: BY_Z[:3], 5: BY_Z[3:]}
NT = (((1,), (1,)), ((), ()))
NN = (((1,), (0,)), ((), ()))
TN = (((0,), (0,)), ((), ()))
F32 = jnp.float32
BF16 = jnp.bfloat16


def dot(a, b, dims):
    return lax.dot_general(a, b, dims, preferred_element_type=F32)


def remote(src, dst, send, recv, device):
    return pltpu.make_async_remote_copy(
        src_ref=src, dst_ref=dst, send_sem=send, recv_sem=recv,
        device_id=device, device_id_type=pl.DeviceIdType.MESH,
    )


def kernel(
    q_in, k_in, v_in, g_in, dq_out, dk_out, dv_out,
    q, g, kv, top, mass, wsum, e_all, tops, ds_all, dqt, dqs, out1, in1, acc, out2, in2, out3, in3, fin,
    own_sem, q_s, q_r, k_s, k_r, z_s, z_r,
    r1_s, r1_r, r2_s, r2_r, r3_s, r3_r, o_s, o_r,
):
    rows = q_in.shape[0]
    pb, kvi = lax.axis_index("pb"), lax.axis_index("kv")
    core, zh = pb % 2, pb // 2
    y, x, zl = kvi // 8, (kvi // 2) % 4, kvi % 2

    def a_peer(d):
        return (pb, (((y + d * (1 - core)) % SIDE) * SIDE + (x + d * core) % SIDE) * 2 + zl)

    def b_peer(d):
        return (pb, (((y + d * core) % SIDE) * SIDE + (x + d * (1 - core)) % SIDE) * 2 + zl)

    twin = (zh * 2 + 1 - core, kvi)
    far_z = (1 - zh) * 2 + core
    near = kvi + 1 - 2 * zl
    z_peer = (pb, near)
    z_peers = ((far_z, kvi), z_peer, (far_z, near))
    mine = pl.ds(pl.multiple_of(core * D, D), D)
    other = pl.ds(pl.multiple_of((1 - core) * D, D), D)

    def slot(sa, sb):
        return kv.at[POS[sa, sb]]

    barrier = pltpu.get_barrier_semaphore()
    peers = [twin, *z_peers]
    peers += [a_peer(d) for d in (1, 2, 3)] + [b_peer(d) for d in (1, 2, 3)]
    for peer in peers:
        pl.semaphore_signal(barrier, inc=1, device_id=peer, device_id_type=pl.DeviceIdType.MESH)

    here = slot(0, 0)
    own = []
    for n, (src, dst) in enumerate((
        (k_in.at[:, mine], here.at[0, 0:D]),
        (v_in.at[:, mine], here.at[1, 0:D]),
        (q_in.at[:, mine], q.at[0:rows]),
        (g_in.at[:, mine], g.at[0:rows]),
    )):
        own.append(pltpu.make_async_copy(src, dst, own_sem.at[n]))
        own[-1].start()
    pl.semaphore_wait(barrier, len(peers))

    sends = []

    def go(*args):
        c = remote(*args)
        c.start()
        sends.append(c)
        return c

    own[0].wait()
    own[1].wait()

    def part(pos, half):
        return kv.at[pos, :, half * D : half * D + D]

    def along_b(s, half):
        at = POS[0, BACK[s]]
        go(
            part(POS[0, 0], half), part(at, half),
            k_s.at[POS[0, s], half], k_r.at[at, half], b_peer(GRAY[s]),
        )

    def along_a(sa, sb, half):
        at = POS[BACK[sa], sb]
        go(
            part(POS[0, sb], half), part(at, half),
            k_s.at[POS[sa, sb], half], k_r.at[at, half], a_peer(GRAY[sa]),
        )

    def z_copy(pos, n):
        return remote(
            kv.at[pos, n, 0:D], kv.at[pos, n, D:HALF], z_s.at[pos, n], z_r.at[pos, n], z_peers[1 + n]
        )

    def along_z(pos):
        for n in (0, 1):
            c = z_copy(pos, n)
            c.start()
            sends.append(c)

    def have(pos, half):
        remote(
            part(pos, half), part(pos, half), k_s.at[pos, half], k_r.at[pos, half], twin
        ).wait_recv()

    def have_z(pos):
        for n in (0, 1):
            z_copy(pos, n).wait_recv()

    for s in (3, 1, 2):
        along_b(s, 0)
    for sa in (3, 1, 2):
        along_a(sa, 0, 0)
    along_z(POS[0, 0])
    q_copies = [
        go(q_in.at[:, other], q.at[rows : 2 * rows], q_s.at[0], q_r.at[0], twin),
        go(g_in.at[:, other], g.at[rows : 2 * rows], q_s.at[1], q_r.at[1], twin),
    ]
    top[...] = jnp.full_like(top, -1e30)
    mass[...] = jnp.zeros_like(mass)
    wsum[...] = jnp.zeros_like(wsum)
    waited = {(0, 0, 0)}

    def need(sa, sb, half):
        if (sa, sb, half) in waited:
            return
        waited.add((sa, sb, half))
        if half and (sa, sb) in ((0, 0), *BY_Z):
            have_z(POS[sa, sb])
        else:
            have(POS[sa, sb], half)

    need(0, 0, 1)
    for s in (3, 1, 2):
        along_b(s, 1)
    for sa in (1, 2, 3):
        along_a(sa, 0, 1)
    for sb in (3, 1, 2):
        need(0, sb, 0)
        for sa in (3, 2, 1):
            along_a(sa, sb, 0)
    own[2].wait()
    own[3].wait()
    for c in q_copies:
        c.wait_recv()

    def chunk(i, which):
        first = 2 * i
        return kv[pl.ds(first, 2), which].reshape(CHUNK, D)

    def stats(halves):
        nq = q.shape[0]
        kc, vc = (
            jnp.concatenate([kv[POS[sa, sb], n, h * D : h * D + D] for sa, sb, h in halves])
            for n in (0, 1)
        )
        s = dot(kc, q[...], NT).reshape(CHUNK // 8, 8, nq)
        dp = dot(vc, g[...], NT).reshape(CHUNK // 8, 8, nq)
        before = top[...]
        peak = jnp.maximum(before, jnp.max(s, axis=0) * SCALE2)
        keep = jnp.exp2(before - peak)
        e = jnp.exp2(s * SCALE2 - peak[None])
        top[...] = peak
        for n, (sa, sb, h) in enumerate(halves):
            e_all[POS[sa, sb], h] = e[n * 16 : n * 16 + 16].reshape(D, nq)
            tops[POS[sa, sb], h] = peak
        mass[...] = mass[...] * keep + jnp.sum(e, axis=0)
        wsum[...] = wsum[...] * keep + jnp.sum(e * dp, axis=0)

    for step, halves in enumerate(SCHEDULE):
        if step == A_STEP:
            for sa, sb in BY_A:
                need(0, sb, 1)
                along_a(sa, sb, 1)
        for sa, sb in Z_STEPS.get(step, ()):
            need(sa, sb, 0)
            along_z(POS[sa, sb])
        for sa, sb, half in halves:
            need(sa, sb, half)
        stats(halves)
    peak = jnp.max(top[...], axis=0, keepdims=True)
    keep = jnp.exp2(top[...] - peak)
    total = jnp.sum(mass[...] * keep, axis=0, keepdims=True)
    weighted = jnp.sum(wsum[...] * keep, axis=0, keepdims=True)
    top[0:1] = peak + jnp.log2(total)
    wsum[0:1] = weighted / total

    def r1_copy(sa, sb):
        at = POS[BACK[sa], sb]
        return remote(
            out1.at[sa - 1, sb], in1.at[BACK[sa] - 1, sb],
            r1_s.at[POS[sa, sb]], r1_r.at[at], a_peer(GRAY[sa]),
        )

    def r1_sum(sb):
        for sa in (1, 2, 3):
            at = POS[sa, sb]
            remote(out1.at[sa - 1, sb], in1.at[sa - 1, sb], r1_s.at[at], r1_r.at[at], twin).wait_recv()
        acc[sb] += in1[0, sb].astype(F32) + in1[1, sb].astype(F32) + in1[2, sb].astype(F32)

    def r2_copy(s):
        return remote(
            out2.at[s - 1], in2.at[BACK[s] - 1], r2_s.at[s - 1], r2_r.at[BACK[s] - 1], b_peer(GRAY[s])
        )

    def key_grads(i, at, size, later):
        nq = q.shape[0]
        qq, gg = q[...], g[...]
        if size == CHUNK:
            kc, vc = chunk(i, 0), chunk(i, 1)
        else:
            kc, vc = kv[2 * i + at // HALF, 0], kv[2 * i + at // HALF, 1]
        pieces = pl.ds(2 * i + at // HALF, size // HALF)
        halves = size // D
        dp = dot(vc, gg, NT)
        factor = jnp.exp2(tops[pieces].reshape(halves, 1, 8, nq) - top[0:1])
        e = e_all[pieces].reshape(halves, D // 8, 8, nq)
        p = (e * factor).reshape(size, nq)
        ds = (p * (dp - wsum[0:1])).astype(BF16)
        if later:
            ds_all[i - LATER, pl.ds(at, size)] = ds
        else:
            dqt[...] += dot(kc, ds, TN)
        return dot(ds, qq, NN) * SCALE, dot(p.astype(BF16), gg, NN)

    def place(sa, sb, both, at):
        for n in (0, 1):
            part = both[n][at : at + HALF]
            if sa:
                out1[sa - 1, sb, n] = part.astype(BF16)
            else:
                acc[sb, n] = part
        if sa:
            r1_copy(sa, sb).start()

    def grads(later, i, carry):
        both = key_grads(i, 0, CHUNK, later)
        for pos, (sa, sb) in enumerate(ORDER[:-2]):
            @pl.when(i == pos // 2)
            def _(pos=pos, sa=sa, sb=sb):
                place(sa, sb, both, (pos % 2) * HALF)

        for at, slots in ((POS[0, 2] // 2, (1, 2)), (POS[0, 3] // 2, (3,))):
            @pl.when(i == at)
            def _(slots=slots):
                for sb in slots:
                    r1_sum(sb)
                    out2[sb - 1] = acc[sb].astype(BF16)
                    r2_copy(sb).start()

        return carry

    dqt[...] = jnp.zeros_like(dqt)
    lax.fori_loop(0, LATER, functools.partial(grads, False), 0)
    def last(n, carry):
        both = key_grads(STEPS - 1, n * HALF, HALF, True)
        for k, (sa, sb) in enumerate(ORDER[-2:]):
            @pl.when(n == k)
            def _(sa=sa, sb=sb):
                place(sa, sb, both, 0)

        return carry

    lax.fori_loop(0, 2, last, 0)

    def make_dq(half):
        size = (STEPS - LATER) * CHUNK
        queries = slice(half * rows, half * rows + rows)
        keys = kv[2 * LATER :, 0].reshape(size, D)
        ds = ds_all[:, :, queries].reshape(size, rows)
        dqs[queries] = (dqt[:, queries] + dot(keys, ds, TN)).T * SCALE

    make_dq(1)
    go(dqs.at[rows : 2 * rows], dq_out.at[:, mine], o_s.at[0], o_r.at[0], twin)
    r1_sum(0)
    for s in (1, 2, 3):
        remote(in2.at[s - 1], in2.at[s - 1], r2_s.at[s - 1], r2_r.at[s - 1], twin).wait_recv()
    fin[...] = acc[0] + in2[0].astype(F32) + in2[1].astype(F32) + in2[2].astype(F32)
    out3[...] = fin[...].astype(BF16)
    z_sums = [
        go(out3.at[:, at : at + D], in3.at[n], r3_s.at[n], r3_r.at[n], z_peers[n])
        for n, at in ((0, 0), (1, D), (2, D))
    ]
    make_dq(0)
    dq_here = pltpu.make_async_copy(dqs.at[0:rows], dq_out.at[:, mine], own_sem.at[0])
    dq_here.start()
    for c in z_sums:
        c.wait_recv()
    fin[:, 0:D] += in3[0].astype(F32) + in3[1].astype(F32) + in3[2].astype(F32)
    outs = [
        go(fin.at[n, 0:D], ref.at[:, mine], o_s.at[n + 1], o_r.at[n + 1], twin)
        for n, ref in enumerate((dk_out, dv_out))
    ]
    local = [
        pltpu.make_async_copy(fin.at[n, 0:D], ref.at[:, mine], own_sem.at[n + 1])
        for n, ref in enumerate((dk_out, dv_out))
    ]
    for c in local:
        c.start()
    for c in (dq_here, *local):
        c.wait()
    remote(dqs.at[0:rows], dq_out.at[:, other], o_s.at[0], o_r.at[0], twin).wait_recv()
    for n, ref in enumerate((dk_out, dv_out)):
        remote(fin.at[n, 0:D], ref.at[:, other], o_s.at[n + 1], o_r.at[n + 1], twin).wait_recv()
    for c in sends:
        c.wait_send()
    for s in (1, 2, 3):
        for sb in range(SIDE):
            r1_copy(s, sb).wait_send()
        r2_copy(s).wait_send()


def hand_over(dq, dk, dv, dq_out, dk_out, dv_out, held, sem_in, sem_out):
    size = held.shape[1]
    places = [(src, dst, 0) for src, dst in ((dk, dk_out), (dv, dv_out))]
    places += [(dq, dq_out, at) for at in range(0, dq.shape[0], size)]
    ins, outs = [], []
    for n, (src, dst, at) in enumerate(places):
        ins.append(pltpu.make_async_copy(src.at[at : at + size], held.at[n], sem_in.at[n]))
        outs.append(pltpu.make_async_copy(held.at[n], dst.at[at : at + size], sem_out.at[n]))
        ins[-1].start()
    for here, there in zip(ins, outs):
        here.wait()
        there.start()
    for there in outs:
        there.wait()


def local(queries, keys, values, dout):
    rows = queries.shape[0]
    key_rows = keys.shape[0]
    dma = pltpu.SemaphoreType.DMA
    vmem = pltpu.VMEM
    blocks = 2 + rows // key_rows
    made = pl.pallas_call(
        kernel,
        out_shape=(
            jax.ShapeDtypeStruct((rows, 2 * D), F32),
            jax.ShapeDtypeStruct((key_rows, 2 * D), F32),
            jax.ShapeDtypeStruct((key_rows, 2 * D), F32),
        ),
        in_specs=[pl.BlockSpec(memory_space=pl.ANY)] * 4,
        out_specs=[pl.BlockSpec(memory_space=pl.ANY)] * 3,
        scratch_shapes=[
            vmem((2 * rows, D), BF16),
            vmem((2 * rows, D), BF16),
            vmem((2 * STEPS, 2, HALF, D), BF16),
            vmem((8, 2 * rows), F32),
            vmem((8, 2 * rows), F32),
            vmem((8, 2 * rows), F32),
            vmem((2 * STEPS, 2, D, 2 * rows), F32),
            vmem((2 * STEPS, 2, 8, 2 * rows), F32),
            vmem((STEPS - LATER, CHUNK, 2 * rows), BF16),
            vmem((D, 2 * rows), F32),
            vmem((2 * rows, D), F32),
            vmem((3, SIDE, 2, HALF, D), BF16),
            vmem((3, SIDE, 2, HALF, D), BF16),
            vmem((SIDE, 2, HALF, D), F32),
            vmem((3, 2, HALF, D), BF16),
            vmem((3, 2, HALF, D), BF16),
            vmem((2, HALF, D), BF16),
            vmem((3, 2, D, D), BF16),
            vmem((2, HALF, D), F32),
            dma((4,)), dma((2,)), dma((2,)),
            dma((2 * STEPS, 2)), dma((2 * STEPS, 2)), dma((2 * STEPS, 2)), dma((2 * STEPS, 2)),
            dma((2 * STEPS,)), dma((2 * STEPS,)), dma((3,)), dma((3,)),
            dma((3,)), dma((3,)), dma((3,)), dma((3,)),
        ],
        compiler_params=pltpu.CompilerParams(
            collective_id=0, has_side_effects=True, vmem_limit_bytes=60 * 2**20
        ),
    )(queries, keys, values, dout)
    return pl.pallas_call(
        hand_over,
        out_shape=tuple(jax.ShapeDtypeStruct(m.shape, m.dtype) for m in made),
        in_specs=[pl.BlockSpec(memory_space=pl.ANY)] * 3,
        out_specs=[pl.BlockSpec(memory_space=pl.ANY)] * 3,
        scratch_shapes=[vmem((blocks, key_rows, 2 * D), F32), dma((blocks,)), dma((blocks,))],
    )(*made)


def solution(mesh):
    return jax.shard_map(
        local,
        mesh=mesh,
        in_specs=(P(("pb", "kv"), None), P("kv", None), P("kv", None), P(("pb", "kv"), None)),
        out_specs=(P(("pb", "kv"), None), P("kv", None), P("kv", None)),
        check_vma=False,
    )
```
